512 devices in a mesh: band: 8 (over y_lo, core), grid: 64 (over y_hi, x, z).
Axes of the slice: x: 4, y: 8 (y_hi: 2, y_lo: 4; y = y_hi * 4 + y_lo), z: 8, core: 2. Of those that a mesh axis runs over, the one named last changes fastest.
Arguments:
- orbitals: float32 [8, 2, 192, 192, 192], P('band', None, 'grid'), may hold values from -6 to 6
- occupations: float32 [8], P('band'), may hold values from 0.5 to 2
- ion_potential: float32 [192, 192, 192], P('grid'), may hold values from -0.6 to 0.6
- hxc_potential: float32 [192, 192, 192], P('grid'), may hold values from -0.4 to 0.4
Outputs:
- new_orbitals: float32 [8, 2, 192, 192, 192], P('band', None, 'grid')
- new_potential: float32 [192, 192, 192], P('grid')
The draws below stay inside these ranges and needn't reach their ends.
All inputs are finite; a program needn't handle non-finite values.
Results may differ from the reference program's by a relative error of at most 0.0003.
Values sent between devices are 32-bit elements; how exact they have to be, the bound alone decides.
A program may use at most 64 MiB of HBM per device.

```python
import math
import jax
import jax.numpy as jnp
from jax import lax

NG = 192
BANDS = 8


def level_of(rng, shape, shards, smallest, top_value):
    loudness = 1.0
    for dim, shards_of in shards:
        heights = jax.random.uniform(jax.random.fold_in(jax.random.fold_in(rng, 6), dim), (shards_of,), jnp.float32, smallest / len(shards), top_value / len(shards))
        loudness = loudness * jnp.repeat(jnp.exp(heights), shape[dim] // shards_of).reshape((-1,) + (1,) * (len(shape) - 1 - dim))
    return loudness


def centred(rng, shape, spread, reach, cuts=(), kind=jnp.bfloat16):
    entries = jax.random.normal(rng, shape, jnp.float32) * spread
    if len(cuts) > 0:
        entries = level_of(rng, shape, cuts, -0.22, 0.18) * entries
    return jnp.clip(entries, min=-reach, max=reach).astype(kind)


def setup_inputs(seed: int = 0) -> dict:
    streams_of = jax.random.split(jax.random.key(seed), 5)
    return {
        "orbitals": centred(streams_of[0], (BANDS, 2, NG, NG, NG), 1.0, 6.0, ((0, 8), (2, 64)), jnp.float32),
        "occupations": jnp.clip(jnp.exp(math.log(2.0) - 1.3862944 * jax.random.uniform(streams_of[1], (BANDS,), jnp.float32) ** level_of(streams_of[1], (BANDS,), ((0, 8),), -0.2, 0.2)), 0.5, 2.0),
        "ion_potential": jnp.clip(jax.random.uniform(streams_of[2], (NG, NG, NG), jnp.float32, -0.6, 0.6) * level_of(streams_of[2], (NG, NG, NG), ((0, 64),), -0.4, 0.0), -0.6, 0.6),
        "hxc_potential": jnp.clip(jax.random.uniform(streams_of[3], (NG, NG, NG), jnp.float32, -0.4, 0.4) * level_of(streams_of[3], (NG, NG, NG), ((0, 64),), -0.4, 0.0), -0.4, 0.4),
    }


BESSEL_ZERO = 0.8462873527504802
BESSEL_ONE = 0.36884204609417703
BESSEL_TWO = 0.07581776248
XC_FACTOR = 0.98474502

def squares_grid():
    idx = jnp.arange(NG, dtype=jnp.int32)
    freq = jnp.where(idx < NG // 2, idx, idx - NG).astype(jnp.float32)
    sq = freq * freq
    return sq[:, None, None] + sq[None, :, None] + sq[None, None, :]

def reference(orbitals, occupations, ion_potential, hxc_potential):
    kk = squares_grid()
    kinetic = 2.0 * kk / (3.0 * (NG / 2) ** 2) - 1.0
    potential = ion_potential + hxc_potential

    def hamilton(field):
        return jnp.fft.ifftn(kinetic * jnp.fft.fftn(field)) + potential * field

    def propagate(orbital):
        psi = orbital[0] + 1j * orbital[1]
        first = hamilton(psi)
        second = 2.0 * hamilton(first) - psi
        fresh = BESSEL_ZERO * psi - 2j * BESSEL_ONE * first - 2.0 * BESSEL_TWO * second
        return jnp.stack([jnp.real(fresh), jnp.imag(fresh)]).astype(jnp.float32)
    new_orbitals = lax.map(propagate, orbitals)
    weights = occupations[:, None, None, None]
    density = lax.optimization_barrier(jnp.sum(weights * (new_orbitals[:, 0] ** 2 + new_orbitals[:, 1] ** 2), axis=0))
    kernel = jnp.where(kk > 0, NG * jnp.sqrt(jnp.float32(NG)) / 16.0 / (kk + 1.0), 0.0)
    hartree = jnp.real(jnp.fft.ifftn(kernel * jnp.fft.fftn(density)))
    new_potential = (hartree - XC_FACTOR * jnp.cbrt(density)).astype(jnp.float32)
    return (new_orbitals, new_potential)
```

```python
import functools
import math

import jax
import jax.numpy as jnp
import numpy as np
from jax import lax
from jax.experimental import pallas as pl
from jax.experimental.pallas import tpu as pltpu
from jax.sharding import PartitionSpec as P

BESSEL_ZERO = 0.8462873527504802
BESSEL_ONE = 0.36884204609417703
BESSEL_TWO = 0.07581776248
XC_FACTOR = 0.98474502
MESH = pl.DeviceIdType.MESH
N = 192
G = 64
SLOT = 40
ROWS = 34
BACK = 32
VROWS = 7


def circulant():
    idx = np.arange(N)
    freq = np.where(idx < N // 2, idx, idx - N).astype(np.float64)
    eigen = 2.0 * freq * freq / (3.0 * (N / 2) ** 2)
    angle = 2.0 * np.pi * ((idx[:, None] * idx[None, :]) % N) / N
    first = (np.cos(angle) @ eigen) / N
    return first[(idx[:, None] - idx[None, :]) % N]


def split_table(table):
    high = table.astype(jnp.bfloat16)
    low = (table - high.astype(np.float64)).astype(jnp.bfloat16)
    return np.stack([high, low])


def halves(value):
    high = value.astype(jnp.bfloat16)
    return high, (value - high.astype(jnp.float32)).astype(jnp.bfloat16)


def dot(a, b):
    return jnp.dot(a, b, preferred_element_type=jnp.float32)


def left_mul(table, value):
    high, low = halves(value)
    return dot(table[0], high) + (dot(table[0], low) + dot(table[1], high))


def right_mul(value, table):
    high, low = halves(value)
    return dot(high, table[0]) + (dot(low, table[0]) + dot(high, table[1]))


def peer(me, d):
    yh, x, z = me // 32, (me // 8) % 4, me % 8
    dy, dx, dz = d // 32, (d // 8) % 4, d % 8
    return ((yh + dy) % 2) * 32 + ((x + dx) % 4) * 8 + (z + dz) % 8


def scatter(me, src, dst, slot, rows, send_sem, recv_sem):
    def send(s, carry):
        to = peer(me, (s * 29) % G)
        pltpu.make_async_remote_copy(
            src_ref=src.at[pl.ds(pl.multiple_of(to * slot, 8), rows)],
            dst_ref=dst.at[pl.ds(pl.multiple_of(me * slot, 8), rows)],
            send_sem=send_sem,
            recv_sem=recv_sem,
            device_id={"grid": to},
            device_id_type=MESH,
        ).start()
        return carry

    lax.fori_loop(1, G, send, 0)


def own(me, src, dst, slot, rows, sem):
    return pltpu.make_async_copy(
        src.at[pl.ds(pl.multiple_of(me * slot, 8), rows)],
        dst.at[pl.ds(pl.multiple_of(me * slot, 8), rows)],
        sem,
    )


def drain(ref, rows, sem):
    span = ref.at[pl.ds(0, (G - 1) * rows)]
    pltpu.make_async_copy(span, span, sem).wait()


def propagate(
    psi, ion, hxc, d_ref, dp_ref, fresh,
    out_a, in_a, out_u, in_u, out_c, in_c, vshare, pot, once, twice,
    send_sems, recv_sems, own_sems,
):
    me = lax.axis_index("grid")
    core = lax.axis_index("band") % 2
    sibling = {"band": lax.axis_index("band") + 1 - 2 * core}

    barrier = pltpu.get_barrier_semaphore()

    def greet(s, carry):
        pl.semaphore_signal(barrier, inc=1, device_id={"grid": peer(me, s)}, device_id_type=MESH)
        return carry

    lax.fori_loop(1, G, greet, 0)
    pl.semaphore_signal(barrier, inc=1, device_id=sibling, device_id_type=MESH)

    blocks = []
    tails = []
    for x in range(3):
        value = ion[x] + hxc[x]
        pot[x] = value - 1.0
        for j in range(3):
            blocks.append(value[64 * j : 64 * j + 64, :128])
            tails.append(value[64 * j : 64 * j + 64, 128:])
    tails.append(tails[8])
    for i in range(5):
        blocks.append(jnp.concatenate([tails[2 * i], tails[2 * i + 1]], axis=1))
    for i in range(VROWS):
        out_a[pl.ds(27 + i, G, stride=SLOT), :] = jnp.where(core == 0, blocks[i], blocks[VROWS + i])
    for x in range(3):
        re, im = psi[0, x], psi[1, x]
        kinds = (re[:, :128], im[:, :128], jnp.concatenate([re[:, 128:], im[:, 128:]], axis=1))
        for kind in range(3):
            for j in range(3):
                out_a[pl.ds(x * 9 + kind * 3 + j, G, stride=SLOT), :] = kinds[kind][64 * j : 64 * j + 64]

    pl.semaphore_wait(barrier, G)
    mine = own(me, out_a, in_a, SLOT, ROWS, own_sems.at[0])
    mine.start()
    scatter(me, out_a, in_a, SLOT, ROWS, send_sems.at[0], recv_sems.at[0])

    def inside(i, carry):
        c, x = i // 3, i % 3
        table = d_ref[...]
        value = psi[c, x]
        v = pot[x]
        a = left_mul(table, value) + right_mul(value, table) + v * value
        once[c, x] = a
        twice[c, x] = left_mul(table, a) + right_mul(a, table) + v * a
        return carry

    lax.fori_loop(0, 6, inside, 0)

    mine.wait()
    drain(in_a, ROWS, recv_sems.at[0])

    for i in range(VROWS):
        vshare[core, pl.ds(64 * i, 64), :] = in_a[pl.ds(27 + i, G, stride=SLOT), :]
    swap = pltpu.make_async_remote_copy(
        src_ref=vshare.at[core],
        dst_ref=vshare.at[core],
        send_sem=send_sems.at[3],
        recv_sem=recv_sems.at[3],
        device_id=sibling,
        device_id_type=MESH,
    )
    swap.start()

    def columns(kind):
        return jnp.concatenate(
            [
                jnp.concatenate(
                    [in_a[pl.ds(x * 9 + kind * 3 + j, G, stride=SLOT), :] for j in range(3)], axis=1
                )
                for x in range(3)
            ],
            axis=0,
        )

    def spread(ref, kind, value):
        for x in range(3):
            for j in range(3):
                ref[pl.ds(x * 9 + kind * 3 + j, G, stride=BACK), :] = value[
                    64 * x : 64 * x + 64, 128 * j : 128 * j + 128
                ]

    table = dp_ref[...]
    for kind in range(3):
        spread(out_u, kind, left_mul(table, columns(kind)))
    mine = own(me, out_u, in_u, BACK, 27, own_sems.at[1])
    mine.start()
    scatter(me, out_u, in_u, BACK, 27, send_sems.at[1], recv_sems.at[1])

    swap.wait()

    def vblock(i):
        half, row = i // VROWS, i % VROWS
        return vshare[half, 64 * row : 64 * row + 64, :]

    def vtail(i):
        pair = vblock(9 + i // 2)
        piece = pair[:, :64] if i % 2 == 0 else pair[:, 64:]
        return jnp.concatenate([piece, piece], axis=1)

    def vcolumns(kind):
        pick = vtail if kind == 2 else vblock
        return jnp.concatenate(
            [jnp.concatenate([pick(3 * x + j) for j in range(3)], axis=1) for x in range(3)], axis=0
        )

    def ucolumns(kind):
        return jnp.concatenate(
            [
                jnp.concatenate(
                    [out_u[pl.ds(x * 9 + kind * 3 + j, G, stride=BACK), :] for j in range(3)], axis=1
                )
                for x in range(3)
            ],
            axis=0,
        )

    for kind in range(3):
        value = ucolumns(kind) + (vcolumns(kind) - 1.0) * columns(kind)
        spread(out_c, kind, left_mul(table, value))
    mine_c = own(me, out_c, in_c, BACK, 27, own_sems.at[2])
    mine_c.start()
    scatter(me, out_c, in_c, BACK, 27, send_sems.at[2], recv_sems.at[2])

    def planes(ref, x):
        kinds = [
            jnp.concatenate(
                [ref[pl.ds(x * 9 + kind * 3 + j, G, stride=BACK), :] for j in range(3)], axis=0
            )
            for kind in range(3)
        ]
        re = jnp.concatenate([kinds[0], kinds[2][:, :64]], axis=1)
        im = jnp.concatenate([kinds[1], kinds[2][:, 64:]], axis=1)
        return re, im

    mine.wait()
    drain(in_u, 27, recv_sems.at[1])
    inner = d_ref[...]
    alpha = BESSEL_ZERO + 2.0 * BESSEL_TWO
    for x in range(3):
        ure, uim = planes(in_u, x)
        v = pot[x]
        second_re = twice[0, x] + 2.0 * (left_mul(inner, ure) + right_mul(ure, inner)) + v * ure
        second_im = twice[1, x] + 2.0 * (left_mul(inner, uim) + right_mul(uim, inner)) + v * uim
        first_re = once[0, x] + ure
        first_im = once[1, x] + uim
        once[0, x] = alpha * psi[0, x] + 2.0 * BESSEL_ONE * first_im - 4.0 * BESSEL_TWO * second_re
        once[1, x] = alpha * psi[1, x] - 2.0 * BESSEL_ONE * first_re - 4.0 * BESSEL_TWO * second_im

    mine_c.wait()
    drain(in_c, 27, recv_sems.at[2])
    for x in range(3):
        cre, cim = planes(in_c, x)
        fresh[0, x] = once[0, x] - 4.0 * BESSEL_TWO * cre
        fresh[1, x] = once[1, x] - 4.0 * BESSEL_TWO * cim

    drain(out_a, ROWS, send_sems.at[0])
    drain(out_u, 27, send_sems.at[1])
    drain(out_c, 27, send_sems.at[2])


def orbitals_step(orbitals, ion, hxc):
    table = circulant()
    order = np.arange(N)
    order = 3 * (order % G) + order // G
    vmem = pl.BlockSpec(memory_space=pltpu.VMEM)
    f32 = jnp.float32
    return pl.pallas_call(
        propagate,
        out_shape=jax.ShapeDtypeStruct((2, 3, N, N), f32),
        in_specs=[vmem] * 5,
        out_specs=vmem,
        scratch_shapes=[
            pltpu.VMEM((G * SLOT, 128), f32),
            pltpu.VMEM((G * SLOT, 128), f32),
            pltpu.VMEM((G * BACK, 128), f32),
            pltpu.VMEM((G * BACK, 128), f32),
            pltpu.VMEM((G * BACK, 128), f32),
            pltpu.VMEM((G * BACK, 128), f32),
            pltpu.VMEM((2, VROWS * 64, 128), f32),
            pltpu.VMEM((3, N, N), f32),
            pltpu.VMEM((2, 3, N, N), f32),
            pltpu.VMEM((2, 3, N, N), f32),
            pltpu.SemaphoreType.DMA((4,)),
            pltpu.SemaphoreType.DMA((4,)),
            pltpu.SemaphoreType.DMA((3,)),
        ],
        compiler_params=pltpu.CompilerParams(
            collective_id=1, has_side_effects=True, vmem_limit_bytes=56 << 20
        ),
        name="propagate",
    )(orbitals, ion, hxc, split_table(table), split_table(table[order][:, order]))


def tables(length):
    idx = jnp.arange(length, dtype=jnp.int32)
    angle = (idx[:, None] * idx[None, :] % length).astype(jnp.float32) * (2.0 * math.pi / length)
    return (jnp.cos(angle), jnp.sin(angle))


def transform(real_part, imag_part, form, inverse, length):
    cosine, sine = tables(length)
    high = lax.Precision.HIGHEST
    rc = jnp.einsum(form, real_part, cosine, precision=high)
    rs = jnp.einsum(form, real_part, sine, precision=high)
    ic = jnp.einsum(form, imag_part, cosine, precision=high)
    isn = jnp.einsum(form, imag_part, sine, precision=high)
    if inverse:
        scale = 1.0 / length
        return ((rc - isn) * scale, (ic + rs) * scale)
    return (rc + isn, ic - rs)


def along_z(real_part, imag_part, inverse):
    return transform(real_part, imag_part, "oxyn,nk->oxyk", inverse, real_part.shape[3])


def along_y(real_part, imag_part, inverse):
    return transform(real_part, imag_part, "oxnz,nk->oxkz", inverse, real_part.shape[2])


def along_x(real_part, imag_part, inverse):
    return transform(real_part, imag_part, "onyz,nk->okyz", inverse, real_part.shape[1])


def forward(real_part, imag_part):
    real_part, imag_part = along_z(real_part, imag_part, False)
    real_part, imag_part = along_y(real_part, imag_part, False)
    real_part, imag_part = (
        lax.all_to_all(real_part, "grid", split_axis=2, concat_axis=1, tiled=True),
        lax.all_to_all(imag_part, "grid", split_axis=2, concat_axis=1, tiled=True),
    )
    return along_x(real_part, imag_part, False)


def backward(real_part, imag_part):
    real_part, imag_part = along_x(real_part, imag_part, True)
    real_part, imag_part = (
        lax.all_to_all(real_part, "grid", split_axis=1, concat_axis=2, tiled=True),
        lax.all_to_all(imag_part, "grid", split_axis=1, concat_axis=2, tiled=True),
    )
    real_part, imag_part = along_y(real_part, imag_part, True)
    real_part, imag_part = along_z(real_part, imag_part, True)
    return (real_part, imag_part)


def frequency(idx, length):
    return jnp.where(idx < length // 2, idx, idx - length).astype(jnp.float32)


def squares_block(x_count, y_start, y_count, length):
    fx = frequency(jnp.arange(x_count, dtype=jnp.int32), length)
    fy = frequency(y_start + jnp.arange(y_count, dtype=jnp.int32), length)
    fz = frequency(jnp.arange(length, dtype=jnp.int32), length)
    return (fx * fx)[:, None, None] + (fy * fy)[None, :, None] + (fz * fz)[None, None, :]


def hartree_filter(squares, length):
    return jnp.where(squares > 0, length * math.sqrt(length) / 16.0 / (squares + 1.0), 0.0)


def local(orbitals, occupations, ion_potential, hxc_potential):
    length = orbitals.shape[-1]
    columns = length // lax.axis_size("grid")
    grid_pos = lax.axis_index("grid")
    squares = squares_block(length, grid_pos * columns, columns, length)
    fresh = orbitals_step(orbitals[0], ion_potential, hxc_potential)
    fresh_re, fresh_im = fresh[None, 0], fresh[None, 1]
    new_orbitals = fresh[None]
    partial_value = jnp.sum(
        occupations[:, None, None, None] * (fresh_re * fresh_re + fresh_im * fresh_im), axis=0
    )
    density = lax.psum(partial_value, "band")
    fre, fim = forward(density[None], jnp.zeros_like(density)[None])
    kernel = hartree_filter(squares, length)
    hart_re, hart_im = backward(kernel * fre, kernel * fim)
    new_potential = hart_re[0] - XC_FACTOR * jnp.cbrt(density)
    return (new_orbitals, new_potential)


def solution(mesh):
    placed = (
        P("band", None, "grid", None, None),
        P("band"),
        P("grid", None, None),
        P("grid", None, None),
    )
    return jax.shard_map(
        local,
        mesh=mesh,
        in_specs=placed,
        out_specs=(P("band", None, "grid", None, None), P("grid", None, None)),
        check_vma=False,
    )
```

```python
import math

import jax
import jax.numpy as jnp
import numpy as np
from jax import lax
from jax.experimental import pallas as pl
from jax.experimental.pallas import tpu as pltpu
from jax.sharding import PartitionSpec as P

BESSEL_ZERO = 0.8462873527504802
BESSEL_ONE = 0.36884204609417703
BESSEL_TWO = 0.07581776248
XC_FACTOR = 0.98474502
MESH = pl.DeviceIdType.MESH
N = 192
G = 64
SLOT = 40
ROWS = 34
BACK = 32
VROWS = 7
SHARE = 40
UNIT = 3 * SHARE
HALF = 4 * UNIT


def circulant():
    idx = np.arange(N)
    freq = np.where(idx < N // 2, idx, idx - N).astype(np.float64)
    eigen = 2.0 * freq * freq / (3.0 * (N / 2) ** 2)
    angle = 2.0 * np.pi * ((idx[:, None] * idx[None, :]) % N) / N
    first = (np.cos(angle) @ eigen) / N
    return first[(idx[:, None] - idx[None, :]) % N]


def hartley():
    idx = np.arange(N)
    angle = 2.0 * np.pi * ((idx[:, None] * idx[None, :]) % N) / N
    return (np.cos(angle) + np.sin(angle)) / math.sqrt(N)


def split_table(table, parts=2):
    pieces = []
    for _ in range(parts):
        piece = table.astype(jnp.bfloat16)
        pieces.append(piece)
        table = table - piece.astype(np.float64)
    return np.stack(pieces)


def halves(value):
    high = value.astype(jnp.bfloat16)
    return high, (value - high.astype(jnp.float32)).astype(jnp.bfloat16)


def dot(a, b):
    return jnp.dot(a, b, preferred_element_type=jnp.float32)


def left_mul(table, value):
    high, low = halves(value)
    return dot(table[0], high) + (dot(table[0], low) + dot(table[1], high))


def right_mul(value, table):
    high, low = halves(value)
    return dot(high, table[0]) + (dot(low, table[0]) + dot(high, table[1]))


def thirds(value):
    high, rest = halves(value)
    left = value - high.astype(jnp.float32)
    return high, rest, (left - rest.astype(jnp.float32)).astype(jnp.bfloat16)


def left_fine(table, value):
    high, mid, low = thirds(value)
    small = dot(table[2], high) + dot(table[1], mid) + dot(table[0], low)
    return dot(table[0], high) + (dot(table[1], high) + dot(table[0], mid) + small)


def right_fine(value, table):
    high, mid, low = thirds(value)
    small = dot(high, table[2]) + dot(mid, table[1]) + dot(low, table[0])
    return dot(high, table[0]) + (dot(high, table[1]) + dot(mid, table[0]) + small)


def frequency(idx):
    return jnp.where(idx < N // 2, idx, idx - N).astype(jnp.float32)


def row_of(device):
    return (device * 9 + 15) // 16


def holds_row(device):
    return (row_of(device) * 16) // 9 == device


def peer(me, d):
    yh, x, z = me // 32, (me // 8) % 4, me % 8
    dy, dx, dz = d // 32, (d // 8) % 4, d % 8
    return ((yh + dy) % 2) * 32 + ((x + dx) % 4) * 8 + (z + dz) % 8


def scatter(me, src, dst, slot, rows, send_sem, recv_sem):
    def send(s, carry):
        to = peer(me, (s * 29) % G)
        pltpu.make_async_remote_copy(
            src_ref=src.at[pl.ds(pl.multiple_of(to * slot, 8), rows)],
            dst_ref=dst.at[pl.ds(pl.multiple_of(me * slot, 8), rows)],
            send_sem=send_sem,
            recv_sem=recv_sem,
            device_id={"grid": to},
            device_id_type=MESH,
        ).start()
        return carry

    lax.fori_loop(1, G, send, 0)


def own(me, src, dst, slot, rows, sem):
    return pltpu.make_async_copy(
        src.at[pl.ds(pl.multiple_of(me * slot, 8), rows)],
        dst.at[pl.ds(pl.multiple_of(me * slot, 8), rows)],
        sem,
    )


def drain(ref, rows, sem):
    span = ref.at[pl.ds(0, (G - 1) * rows)]
    pltpu.make_async_copy(span, span, sem).wait()


def propagate(
    psi, occ, ion, hxc, d_ref, dp_ref, h_ref, hx_ref, hxt_ref, fresh, new_pot,
    out_a, in_a, out_u, in_u, out_c, in_c, vshare, pot, once, twice,
    pairs, part_s, part_r, core_s, core_r, runs_s, runs_r, from_s, from_r,
    to_rows, at_rows, back_rows, got_rows, all_s, all_r,
    send_sems, recv_sems, own_sems, band_send, band_recv,
):
    me = lax.axis_index("grid")
    band = lax.axis_index("band")
    core = band % 2
    line = band // 2
    sibling = {"band": band + 1 - 2 * core}
    others = [(line + d) % 4 for d in range(1, 4)]

    barrier = pltpu.get_barrier_semaphore()

    def greet(s, carry):
        pl.semaphore_signal(barrier, inc=1, device_id={"grid": peer(me, s)}, device_id_type=MESH)
        return carry

    lax.fori_loop(1, G, greet, 0)
    pl.semaphore_signal(barrier, inc=1, device_id=sibling, device_id_type=MESH)
    for other in others:
        pl.semaphore_signal(
            barrier, inc=1, device_id={"band": 2 * other + core}, device_id_type=MESH
        )

    blocks = []
    tails = []
    for x in range(3):
        value = ion[x] + hxc[x]
        pot[x] = value - 1.0
        for j in range(3):
            blocks.append(value[64 * j : 64 * j + 64, :128])
            tails.append(value[64 * j : 64 * j + 64, 128:])
    tails.append(tails[8])
    for i in range(5):
        blocks.append(jnp.concatenate([tails[2 * i], tails[2 * i + 1]], axis=1))
    for i in range(VROWS):
        out_a[pl.ds(27 + i, G, stride=SLOT), :] = jnp.where(core == 0, blocks[i], blocks[VROWS + i])
    for x in range(3):
        re, im = psi[0, x], psi[1, x]
        kinds = (re[:, :128], im[:, :128], jnp.concatenate([re[:, 128:], im[:, 128:]], axis=1))
        for kind in range(3):
            for j in range(3):
                out_a[pl.ds(x * 9 + kind * 3 + j, G, stride=SLOT), :] = kinds[kind][64 * j : 64 * j + 64]

    pl.semaphore_wait(barrier, G + 3)
    mine = own(me, out_a, in_a, SLOT, ROWS, own_sems.at[0])
    mine.start()
    scatter(me, out_a, in_a, SLOT, ROWS, send_sems.at[0], recv_sems.at[0])

    def inside(i, carry):
        c, x = i // 3, i % 3
        table = d_ref[...]
        value = psi[c, x]
        v = pot[x]
        a = left_mul(table, value) + right_mul(value, table) + v * value
        once[c, x] = a
        twice[c, x] = left_mul(table, a) + right_mul(a, table) + v * a
        return carry

    lax.fori_loop(0, 6, inside, 0)

    mine.wait()
    drain(in_a, ROWS, recv_sems.at[0])

    for i in range(VROWS):
        vshare[core, pl.ds(64 * i, 64), :] = in_a[pl.ds(27 + i, G, stride=SLOT), :]
    swap = pltpu.make_async_remote_copy(
        src_ref=vshare.at[core],
        dst_ref=vshare.at[core],
        send_sem=send_sems.at[3],
        recv_sem=recv_sems.at[3],
        device_id=sibling,
        device_id_type=MESH,
    )
    swap.start()

    def columns(kind):
        return jnp.concatenate(
            [
                jnp.concatenate(
                    [in_a[pl.ds(x * 9 + kind * 3 + j, G, stride=SLOT), :] for j in range(3)], axis=1
                )
                for x in range(3)
            ],
            axis=0,
        )

    def spread(ref, kind, value):
        for x in range(3):
            for j in range(3):
                ref[pl.ds(x * 9 + kind * 3 + j, G, stride=BACK), :] = value[
                    64 * x : 64 * x + 64, 128 * j : 128 * j + 128
                ]

    table = dp_ref[...]
    for kind in range(3):
        spread(out_u, kind, left_mul(table, columns(kind)))
    mine = own(me, out_u, in_u, BACK, 27, own_sems.at[1])
    mine.start()
    scatter(me, out_u, in_u, BACK, 27, send_sems.at[1], recv_sems.at[1])

    swap.wait()

    def vblock(i):
        half, row = i // VROWS, i % VROWS
        return vshare[half, 64 * row : 64 * row + 64, :]

    def vtail(i):
        pair = vblock(9 + i // 2)
        piece = pair[:, :64] if i % 2 == 0 else pair[:, 64:]
        return jnp.concatenate([piece, piece], axis=1)

    def vcolumns(kind):
        pick = vtail if kind == 2 else vblock
        return jnp.concatenate(
            [jnp.concatenate([pick(3 * x + j) for j in range(3)], axis=1) for x in range(3)], axis=0
        )

    def ucolumns(kind):
        return jnp.concatenate(
            [
                jnp.concatenate(
                    [out_u[pl.ds(x * 9 + kind * 3 + j, G, stride=BACK), :] for j in range(3)], axis=1
                )
                for x in range(3)
            ],
            axis=0,
        )

    for kind in range(3):
        value = ucolumns(kind) + (vcolumns(kind) - 1.0) * columns(kind)
        spread(out_c, kind, left_mul(table, value))
    mine_c = own(me, out_c, in_c, BACK, 27, own_sems.at[2])
    mine_c.start()
    scatter(me, out_c, in_c, BACK, 27, send_sems.at[2], recv_sems.at[2])

    def planes(ref, x):
        kinds = [
            jnp.concatenate(
                [ref[pl.ds(x * 9 + kind * 3 + j, G, stride=BACK), :] for j in range(3)], axis=0
            )
            for kind in range(3)
        ]
        re = jnp.concatenate([kinds[0], kinds[2][:, :64]], axis=1)
        im = jnp.concatenate([kinds[1], kinds[2][:, 64:]], axis=1)
        return re, im

    mine.wait()
    drain(in_u, 27, recv_sems.at[1])
    inner = d_ref[...]
    alpha = BESSEL_ZERO + 2.0 * BESSEL_TWO
    for x in range(3):
        ure, uim = planes(in_u, x)
        v = pot[x]
        second_re = twice[0, x] + 2.0 * (left_mul(inner, ure) + right_mul(ure, inner)) + v * ure
        second_im = twice[1, x] + 2.0 * (left_mul(inner, uim) + right_mul(uim, inner)) + v * uim
        first_re = once[0, x] + ure
        first_im = once[1, x] + uim
        once[0, x] = alpha * psi[0, x] + 2.0 * BESSEL_ONE * first_im - 4.0 * BESSEL_TWO * second_re
        once[1, x] = alpha * psi[1, x] - 2.0 * BESSEL_ONE * first_re - 4.0 * BESSEL_TWO * second_im

    mine_c.wait()
    drain(in_c, 27, recv_sems.at[2])
    table_h = h_ref[...]
    weight = occ[0]

    def pack(ref, x, value):
        pairs[...] = jnp.concatenate([value[:96, 128:], value[96:, 128:]], axis=1)
        for b in range(8):
            base = (((b % 2) * 4 + b // 2) * 3 + x) * SHARE
            ref[base : base + 24, :] = value[24 * b : 24 * b + 24, :128]
            ref[base + 24 : base + 36, :] = pairs[12 * b : 12 * b + 12, :]
            ref[base + 36 : base + 40, :] = jnp.zeros((4, 128), jnp.float32)

    for x in range(3):
        cre, cim = planes(in_c, x)
        re = once[0, x] - 4.0 * BESSEL_TWO * cre
        im = once[1, x] - 4.0 * BESSEL_TWO * cim
        fresh[0, x] = re
        fresh[1, x] = im
        rho = weight * (re * re + im * im)
        pack(part_r, x, rho)
        pack(part_s, x, right_fine(left_fine(table_h, rho), table_h))

    def swap_half(src, dst, k):
        half = pl.multiple_of((1 - core) * HALF, 8)
        copy = pltpu.make_async_remote_copy(
            src_ref=src.at[pl.ds(half, HALF)],
            dst_ref=dst,
            send_sem=band_send.at[k],
            recv_sem=band_recv.at[k],
            device_id=sibling,
            device_id_type=MESH,
        )
        copy.start()
        return copy

    def add_half(src, dst, out):
        out[...] = src[pl.ds(pl.multiple_of(core * HALF, 8), HALF), :] + dst[...]

    def to_lines(src, dst, k):
        copies = []
        for i, other in enumerate(others):
            copy = pltpu.make_async_remote_copy(
                src_ref=src.at[pl.ds(pl.multiple_of(other * UNIT, 8), UNIT)],
                dst_ref=dst.at[pl.ds(pl.multiple_of(line * UNIT, 8), UNIT)],
                send_sem=band_send.at[k + i],
                recv_sem=band_recv.at[k + i],
                device_id={"band": 2 * other + core},
                device_id_type=MESH,
            )
            copy.start()
            copies.append(copy)
        mine = pl.ds(pl.multiple_of(line * UNIT, 8), UNIT)
        dst[mine, :] = src[mine, :]
        return copies

    def total(ref):
        return (ref[0:UNIT, :] + ref[UNIT : 2 * UNIT, :]) + (
            ref[2 * UNIT : 3 * UNIT, :] + ref[3 * UNIT : 4 * UNIT, :]
        )

    swap_s = swap_half(part_s, core_s, 0)
    swap_r = swap_half(part_r, core_r, 1)
    swap_s.wait()
    add_half(part_s, core_s, runs_s)
    lines_s = to_lines(runs_s, from_s, 2)
    swap_r.wait()
    add_half(part_r, core_r, runs_r)
    lines_r = to_lines(runs_r, from_r, 5)
    for copy in lines_s:
        copy.wait()

    share = total(from_s)
    for x in range(3):
        to_rows[pl.ds(x, SHARE, stride=8), :] = share[SHARE * x : SHARE * x + SHARE]
    row = row_of(me)
    holder = holds_row(me)

    def send_row(s, carry):
        to = peer(me, (s * 29) % G)

        @pl.when(holds_row(to))
        def _():
            pltpu.make_async_remote_copy(
                src_ref=to_rows.at[pl.ds(pl.multiple_of(row_of(to) * 8, 8), 3)],
                dst_ref=at_rows.at[pl.ds(pl.multiple_of(me * 8, 8), 3)],
                send_sem=send_sems.at[4],
                recv_sem=recv_sems.at[4],
                device_id={"grid": to},
                device_id_type=MESH,
            ).start()

        return carry

    lax.fori_loop(1, G, send_row, 0)

    for copy in lines_r:
        copy.wait()

    def gather_start(ref, k):
        mine = ref.at[pl.ds(pl.multiple_of(core * HALF + line * UNIT, 8), UNIT)]
        copies = []
        for i, other in enumerate(others):
            copy = pltpu.make_async_remote_copy(
                src_ref=mine,
                dst_ref=mine,
                send_sem=band_send.at[k + i],
                recv_sem=band_recv.at[k + i],
                device_id={"band": 2 * other + core},
                device_id_type=MESH,
            )
            copy.start()
            copies.append(copy)
        return copies

    def gather_cores(ref, k):
        half = ref.at[pl.ds(pl.multiple_of(core * HALF, 8), HALF)]
        copy = pltpu.make_async_remote_copy(
            src_ref=half,
            dst_ref=half,
            send_sem=band_send.at[k],
            recv_sem=band_recv.at[k],
            device_id=sibling,
            device_id_type=MESH,
        )
        copy.start()
        return copy

    place = pl.ds(pl.multiple_of(core * HALF + line * UNIT, 8), UNIT)
    rho_share = total(from_r)
    root = jnp.exp(jnp.log(jnp.maximum(rho_share, 1e-37)) * (1.0 / 3.0))
    all_r[place, :] = -XC_FACTOR * jnp.where(rho_share > 0, root, 0.0)
    gather_r = gather_start(all_r, 8)

    @pl.when(holder)
    def _():
        at_rows[pl.ds(pl.multiple_of(me * 8, 8), 8), :] = to_rows[
            pl.ds(pl.multiple_of(row * 8, 8), 8), :
        ]
        drain(at_rows, 3, recv_sems.at[4])
        lines = jnp.concatenate([at_rows[pl.ds(x, G, stride=8), :] for x in range(3)], axis=0)
        spectrum = left_fine(hx_ref[...], lines)
        kx = lax.broadcasted_iota(jnp.int32, (N, 128), 0)
        lane = lax.broadcasted_iota(jnp.int32, (N, 128), 1)
        pair = 12 * band + row - 24
        wide = row < 24
        right = lane >= 64
        ky = jnp.where(wide, 24 * band + row, jnp.where(right, pair + 96, pair))
        kz = jnp.where(wide, lane, jnp.where(right, lane + 64, lane + 128))
        fx, fy, fz = frequency(kx), frequency(ky), frequency(kz)
        kk = fx * fx + fy * fy + fz * fz
        kernel = jnp.where(kk > 0, (N * math.sqrt(N) / 16.0) / (kk + 1.0), 0.0)
        result = left_mul(hxt_ref[...], kernel * spectrum)
        for x in range(3):
            back_rows[pl.ds(x, G, stride=8), :] = result[64 * x : 64 * x + 64]

        def send_back(s, carry):
            to = peer(me, (s * 29) % G)
            pltpu.make_async_remote_copy(
                src_ref=back_rows.at[pl.ds(pl.multiple_of(to * 8, 8), 3)],
                dst_ref=got_rows.at[pl.ds(pl.multiple_of(row * 8, 8), 3)],
                send_sem=send_sems.at[5],
                recv_sem=recv_sems.at[5],
                device_id={"grid": to},
                device_id_type=MESH,
            ).start()
            return carry

        lax.fori_loop(1, G, send_back, 0)
        got_rows[pl.ds(pl.multiple_of(row * 8, 8), 8), :] = back_rows[
            pl.ds(pl.multiple_of(me * 8, 8), 8), :
        ]

    def drain_rows(sem):
        @pl.when(holder)
        def _():
            span = to_rows.at[pl.ds(0, 35 * 3)]
            pltpu.make_async_copy(span, span, sem).wait()

        @pl.when(jnp.logical_not(holder))
        def _():
            span = to_rows.at[pl.ds(0, 36 * 3)]
            pltpu.make_async_copy(span, span, sem).wait()

    for copy in gather_r:
        copy.wait()
    cores_r = gather_cores(all_r, 11)

    drain_rows(recv_sems.at[5])
    for x in range(3):
        all_s[pl.ds(pl.multiple_of(core * HALF + line * UNIT + SHARE * x, 8), SHARE), :] = got_rows[
            pl.ds(x, SHARE, stride=8), :
        ]
    for copy in gather_start(all_s, 12):
        copy.wait()
    cores_r.wait()
    gather_cores(all_s, 15).wait()

    def unpack(ref, x):
        wide = []
        for b in range(8):
            base = (((b % 2) * 4 + b // 2) * 3 + x) * SHARE
            wide.append(ref[base : base + 24, :])
            pairs[12 * b : 12 * b + 12, :] = ref[base + 24 : base + 36, :]
        tail = pairs[...]
        tail = jnp.concatenate([tail[:, :64], tail[:, 64:]], axis=0)
        return jnp.concatenate([jnp.concatenate(wide, axis=0), tail], axis=1)

    for x in range(3):
        spectrum = unpack(all_s, x)
        new_pot[x] = right_mul(left_mul(table_h, spectrum), table_h) + unpack(all_r, x)

    drain(out_a, ROWS, send_sems.at[0])
    drain(out_u, 27, send_sems.at[1])
    drain(out_c, 27, send_sems.at[2])
    drain_rows(send_sems.at[4])

    @pl.when(holder)
    def _():
        drain(back_rows, 3, send_sems.at[5])


def local(orbitals, occupations, ion, hxc):
    table = circulant()
    cas = hartley()
    order = np.arange(N)
    order = 3 * (order % G) + order // G
    vmem = pl.BlockSpec(memory_space=pltpu.VMEM)
    f32 = jnp.float32
    slots = lambda rows: pltpu.VMEM((rows, 128), f32)
    fresh, new_pot = pl.pallas_call(
        propagate,
        out_shape=(jax.ShapeDtypeStruct((2, 3, N, N), f32), jax.ShapeDtypeStruct((3, N, N), f32)),
        in_specs=[vmem, pl.BlockSpec(memory_space=pltpu.SMEM)] + [vmem] * 7,
        out_specs=(vmem, vmem),
        scratch_shapes=[
            slots(G * SLOT),
            slots(G * SLOT),
            slots(G * BACK),
            slots(G * BACK),
            slots(G * BACK),
            slots(G * BACK),
            pltpu.VMEM((2, VROWS * 64, 128), f32),
            pltpu.VMEM((3, N, N), f32),
            pltpu.VMEM((2, 3, N, N), f32),
            pltpu.VMEM((2, 3, N, N), f32),
            slots(96),
            slots(2 * HALF),
            slots(2 * HALF),
            slots(HALF),
            slots(HALF),
            slots(HALF),
            slots(HALF),
            slots(HALF),
            slots(HALF),
            slots(SHARE * 8),
            slots(G * 8),
            slots(G * 8),
            slots(SHARE * 8),
            slots(2 * HALF),
            slots(2 * HALF),
            pltpu.SemaphoreType.DMA((6,)),
            pltpu.SemaphoreType.DMA((6,)),
            pltpu.SemaphoreType.DMA((3,)),
            pltpu.SemaphoreType.DMA((16,)),
            pltpu.SemaphoreType.DMA((16,)),
        ],
        compiler_params=pltpu.CompilerParams(
            collective_id=1, has_side_effects=True, vmem_limit_bytes=56 << 20
        ),
        name="propagate",
    )(
        orbitals[0],
        occupations,
        ion,
        hxc,
        split_table(table),
        split_table(table[order][:, order]),
        split_table(cas, 3),
        split_table(cas[:, order], 3),
        split_table(cas[:, order].T),
    )
    return fresh[None], new_pot


def solution(mesh):
    placed = (
        P("band", None, "grid", None, None),
        P("band"),
        P("grid", None, None),
        P("grid", None, None),
    )
    return jax.shard_map(
        local,
        mesh=mesh,
        in_specs=placed,
        out_specs=(P("band", None, "grid", None, None), P("grid", None, None)),
        check_vma=False,
    )
```

```python
import math

import jax
import jax.numpy as jnp
import numpy as np
from jax import lax
from jax.experimental import pallas as pl
from jax.experimental.pallas import tpu as pltpu
from jax.sharding import PartitionSpec as P

BESSEL_ZERO = 0.8462873527504802
BESSEL_ONE = 0.36884204609417703
BESSEL_TWO = 0.07581776248
XC_FACTOR = 0.98474502
MESH = pl.DeviceIdType.MESH
N = 192
G = 64
SLOT = 40
WIDE = 18
TAIL = 24
VROWS = 7
SHARE = 40
UNIT = 3 * SHARE
HALF = 4 * UNIT


def circulant():
    idx = np.arange(N)
    freq = np.where(idx < N // 2, idx, idx - N).astype(np.float64)
    eigen = 2.0 * freq * freq / (3.0 * (N / 2) ** 2)
    angle = 2.0 * np.pi * ((idx[:, None] * idx[None, :]) % N) / N
    first = (np.cos(angle) @ eigen) / N
    return first[(idx[:, None] - idx[None, :]) % N]


def hartley():
    idx = np.arange(N)
    angle = 2.0 * np.pi * ((idx[:, None] * idx[None, :]) % N) / N
    return (np.cos(angle) + np.sin(angle)) / math.sqrt(N)


def split_table(table, parts=2):
    pieces = []
    for _ in range(parts):
        piece = table.astype(jnp.bfloat16)
        pieces.append(piece)
        table = table - piece.astype(np.float64)
    return np.stack(pieces)


def halves(value):
    high = value.astype(jnp.bfloat16)
    return high, (value - high.astype(jnp.float32)).astype(jnp.bfloat16)


def dot(a, b):
    return jnp.dot(a, b, preferred_element_type=jnp.float32)


def left_mul(table, value):
    high, low = halves(value)
    return dot(table[0], high) + (dot(table[0], low) + dot(table[1], high))


def right_mul(value, table):
    high, low = halves(value)
    return dot(high, table[0]) + (dot(low, table[0]) + dot(high, table[1]))


def thirds(value):
    high, rest = halves(value)
    left = value - high.astype(jnp.float32)
    return high, rest, (left - rest.astype(jnp.float32)).astype(jnp.bfloat16)


def left_fine(table, value):
    high, mid, low = thirds(value)
    small = dot(table[2], high) + dot(table[1], mid) + dot(table[0], low)
    return dot(table[0], high) + (dot(table[1], high) + dot(table[0], mid) + small)


def right_fine(value, table):
    high, mid, low = thirds(value)
    small = dot(high, table[2]) + dot(mid, table[1]) + dot(low, table[0])
    return dot(high, table[0]) + (dot(high, table[1]) + dot(mid, table[0]) + small)


def frequency(idx):
    return jnp.where(idx < N // 2, idx, idx - N).astype(jnp.float32)


def peers(me):
    yh, x, z = me // 32, (me // 8) % 4, me % 8
    planes = [((yh + i % 2) % 2) * 32 + ((x + i // 2) % 4) * 8 for i in range(8)]
    return planes, z


def for_peers(me, act):
    planes, z = peers(me)
    for i in range(1, 8):
        act(planes[i] + z)

    def step(s, carry):
        at = (z + 5 * s) % 8
        for i in range(8):
            act(planes[i] + at)
        return carry

    lax.fori_loop(1, 8, step, 0)


def scatter(me, src, dst, first, rows, send_sem, recv_sem):
    landing = dst.at[pl.ds(pl.multiple_of(me * SLOT + first, 8), rows)]

    def send(to):
        pltpu.make_async_remote_copy(
            src_ref=src.at[pl.ds(pl.multiple_of(to * SLOT + first, 8), rows)],
            dst_ref=landing,
            send_sem=send_sem,
            recv_sem=recv_sem,
            device_id={"grid": to},
            device_id_type=MESH,
        ).start()

    for_peers(me, send)


def own(me, src, dst, first, rows, sem):
    copy = pltpu.make_async_copy(
        src.at[pl.ds(pl.multiple_of(me * SLOT + first, 8), rows)],
        dst.at[pl.ds(pl.multiple_of(me * SLOT + first, 8), rows)],
        sem,
    )
    copy.start()
    return copy


def drain(ref, rows, sem):
    span = ref.at[pl.ds(0, (G - 1) * rows)]
    pltpu.make_async_copy(span, span, sem).wait()


def propagate(
    psi_in, occ, ion_in, hxc_in, d_in, dp_in, h_in, hx_in, hxt_in, fresh_out, new_pot,
    psi, ion, hxc, d_ref, dp_ref, h_ref, hx_ref, hxt_ref, fresh,
    out_a, in_a, out_u, in_u, out_c, in_c, vshare, pot, once, twice,
    pairs, part_s, part_r, core_s, core_r, runs_s, runs_r, from_s, from_r,
    to_rows, at_rows, back_rows, got_rows, all_s, all_r,
    send_sems, recv_sems, own_sems, load_sems, band_send, band_recv,
):
    me = lax.axis_index("grid")
    band = lax.axis_index("band")
    core = band % 2
    line = band // 2
    sibling = {"band": band + 1 - 2 * core}
    others = [(line + d) % 4 for d in range(1, 4)]

    loads = [
        pltpu.make_async_copy(src, dst, load_sems.at[i])
        for i, (src, dst) in enumerate(
            [
                (ion_in, ion),
                (hxc_in, hxc),
                (psi_in.at[0], psi),
                (d_in, d_ref),
                (dp_in, dp_ref),
                (h_in, h_ref),
                (hx_in, hx_ref),
                (hxt_in, hxt_ref),
            ]
        )
    ]
    for load in loads:
        load.start()

    barrier = pltpu.get_barrier_semaphore()

    def greet(to):
        pl.semaphore_signal(barrier, inc=1, device_id={"grid": to}, device_id_type=MESH)

    for_peers(me, greet)
    pl.semaphore_signal(barrier, inc=1, device_id=sibling, device_id_type=MESH)
    for other in others:
        pl.semaphore_signal(
            barrier, inc=1, device_id={"band": 2 * other + core}, device_id_type=MESH
        )

    loads[0].wait()
    loads[1].wait()
    blocks = []
    tails = []
    for x in range(3):
        value = ion[x] + hxc[x]
        pot[x] = value - 1.0
        for j in range(3):
            blocks.append(value[64 * j : 64 * j + 64, :128])
            tails.append(value[64 * j : 64 * j + 64, 128:])
    tails.append(tails[8])
    for i in range(5):
        blocks.append(jnp.concatenate([tails[2 * i], tails[2 * i + 1]], axis=1))
    for i in range(VROWS):
        out_a[pl.ds(TAIL + 9 + i, G, stride=SLOT), :] = jnp.where(core == 0, blocks[i], blocks[VROWS + i])

    def at(x, kind, j):
        return (TAIL if kind == 2 else 9 * kind) + 3 * x + j

    loads[2].wait()
    for x in range(3):
        re, im = psi[0, x], psi[1, x]
        kinds = (re[:, :128], im[:, :128], jnp.concatenate([re[:, 128:], im[:, 128:]], axis=1))
        for kind in range(3):
            for j in range(3):
                out_a[pl.ds(at(x, kind, j), G, stride=SLOT), :] = kinds[kind][64 * j : 64 * j + 64]

    pl.semaphore_wait(barrier, G + 3)
    last = 9 + VROWS
    mine_wide = own(me, out_a, in_a, 0, WIDE, own_sems.at[0])
    mine_tail = own(me, out_a, in_a, TAIL, last, own_sems.at[1])
    scatter(me, out_a, in_a, 0, WIDE, send_sems.at[0], recv_sems.at[0])
    scatter(me, out_a, in_a, TAIL, last, send_sems.at[1], recv_sems.at[1])
    for load in loads[3:]:
        load.wait()

    def inside(i, carry):
        c, x = i // 3, i % 3
        table = d_ref[...]
        value = psi[c, x]
        v = pot[x]
        a = left_mul(table, value) + right_mul(value, table) + v * value
        once[c, x] = a
        twice[c, x] = left_mul(table, a) + right_mul(a, table) + v * a
        return carry

    lax.fori_loop(0, 6, inside, 0)

    def columns(ref, kind):
        return jnp.concatenate(
            [
                jnp.concatenate(
                    [ref[pl.ds(at(x, kind, j), G, stride=SLOT), :] for j in range(3)], axis=1
                )
                for x in range(3)
            ],
            axis=0,
        )

    def spread(ref, kind, value):
        for x in range(3):
            for j in range(3):
                ref[pl.ds(at(x, kind, j), G, stride=SLOT), :] = value[
                    64 * x : 64 * x + 64, 128 * j : 128 * j + 128
                ]

    table = dp_ref[...]
    mine_wide.wait()
    drain(in_a, WIDE, recv_sems.at[0])
    for kind in range(2):
        spread(out_u, kind, left_mul(table, columns(in_a, kind)))
    mine_wide = own(me, out_u, in_u, 0, WIDE, own_sems.at[2])
    scatter(me, out_u, in_u, 0, WIDE, send_sems.at[2], recv_sems.at[2])

    mine_tail.wait()
    drain(in_a, last, recv_sems.at[1])
    spread(out_u, 2, left_mul(table, columns(in_a, 2)))
    mine_tail = own(me, out_u, in_u, TAIL, 9, own_sems.at[3])
    scatter(me, out_u, in_u, TAIL, 9, send_sems.at[3], recv_sems.at[3])

    for i in range(VROWS):
        vshare[core, pl.ds(64 * i, 64), :] = in_a[pl.ds(TAIL + 9 + i, G, stride=SLOT), :]
    swap = pltpu.make_async_remote_copy(
        src_ref=vshare.at[core],
        dst_ref=vshare.at[core],
        send_sem=send_sems.at[6],
        recv_sem=recv_sems.at[6],
        device_id=sibling,
        device_id_type=MESH,
    )
    swap.start()
    swap.wait()

    def vblock(i):
        half, row = i // VROWS, i % VROWS
        return vshare[half, 64 * row : 64 * row + 64, :]

    def vtail(i):
        pair = vblock(9 + i // 2)
        piece = pair[:, :64] if i % 2 == 0 else pair[:, 64:]
        return jnp.concatenate([piece, piece], axis=1)

    def vcolumns(kind):
        pick = vtail if kind == 2 else vblock
        return jnp.concatenate(
            [jnp.concatenate([pick(3 * x + j) for j in range(3)], axis=1) for x in range(3)], axis=0
        )

    for kind in range(3):
        value = columns(out_u, kind) + (vcolumns(kind) - 1.0) * columns(in_a, kind)
        spread(out_c, kind, left_mul(table, value))
    mine_c = [
        own(me, out_c, in_c, 0, WIDE, own_sems.at[4]),
        own(me, out_c, in_c, TAIL, 9, own_sems.at[5]),
    ]
    scatter(me, out_c, in_c, 0, WIDE, send_sems.at[4], recv_sems.at[4])
    scatter(me, out_c, in_c, TAIL, 9, send_sems.at[5], recv_sems.at[5])

    def planes(ref, x):
        kinds = [
            jnp.concatenate(
                [ref[pl.ds(at(x, kind, j), G, stride=SLOT), :] for j in range(3)], axis=0
            )
            for kind in range(3)
        ]
        re = jnp.concatenate([kinds[0], kinds[2][:, :64]], axis=1)
        im = jnp.concatenate([kinds[1], kinds[2][:, 64:]], axis=1)
        return re, im

    mine_wide.wait()
    mine_tail.wait()
    drain(in_u, WIDE, recv_sems.at[2])
    drain(in_u, 9, recv_sems.at[3])
    inner = d_ref[...]
    alpha = BESSEL_ZERO + 2.0 * BESSEL_TWO
    for x in range(3):
        ure, uim = planes(in_u, x)
        v = pot[x]
        second_re = twice[0, x] + 2.0 * (left_mul(inner, ure) + right_mul(ure, inner)) + v * ure
        second_im = twice[1, x] + 2.0 * (left_mul(inner, uim) + right_mul(uim, inner)) + v * uim
        first_re = once[0, x] + ure
        first_im = once[1, x] + uim
        once[0, x] = alpha * psi[0, x] + 2.0 * BESSEL_ONE * first_im - 4.0 * BESSEL_TWO * second_re
        once[1, x] = alpha * psi[1, x] - 2.0 * BESSEL_ONE * first_re - 4.0 * BESSEL_TWO * second_im

    for copy in mine_c:
        copy.wait()
    drain(in_c, WIDE, recv_sems.at[4])
    drain(in_c, 9, recv_sems.at[5])
    table_h = h_ref[...]
    weight = occ[0]

    def pack(ref, x, value):
        pairs[...] = jnp.concatenate([value[:96, 128:], value[96:, 128:]], axis=1)
        for b in range(8):
            base = (((b % 2) * 4 + b // 2) * 3 + x) * SHARE
            ref[base : base + 24, :] = value[24 * b : 24 * b + 24, :128]
            ref[base + 24 : base + 36, :] = pairs[12 * b : 12 * b + 12, :]
            ref[base + 36 : base + 40, :] = jnp.zeros((4, 128), jnp.float32)

    for x in range(3):
        cre, cim = planes(in_c, x)
        re = once[0, x] - 4.0 * BESSEL_TWO * cre
        im = once[1, x] - 4.0 * BESSEL_TWO * cim
        fresh[0, x] = re
        fresh[1, x] = im
        rho = weight * (re * re + im * im)
        pack(part_r, x, rho)
        pack(part_s, x, right_fine(left_fine(table_h, rho), table_h))

    store = pltpu.make_async_copy(fresh, fresh_out.at[0], load_sems.at[8])
    store.start()

    def swap_half(src, dst, k):
        half = pl.multiple_of((1 - core) * HALF, 8)
        copy = pltpu.make_async_remote_copy(
            src_ref=src.at[pl.ds(half, HALF)],
            dst_ref=dst,
            send_sem=band_send.at[k],
            recv_sem=band_recv.at[k],
            device_id=sibling,
            device_id_type=MESH,
        )
        copy.start()
        return copy

    def add_half(src, dst, out):
        out[...] = src[pl.ds(pl.multiple_of(core * HALF, 8), HALF), :] + dst[...]

    def to_lines(src, dst, k):
        copies = []
        for i, other in enumerate(others):
            copy = pltpu.make_async_remote_copy(
                src_ref=src.at[pl.ds(pl.multiple_of(other * UNIT, 8), UNIT)],
                dst_ref=dst.at[pl.ds(pl.multiple_of(line * UNIT, 8), UNIT)],
                send_sem=band_send.at[k + i],
                recv_sem=band_recv.at[k + i],
                device_id={"band": 2 * other + core},
                device_id_type=MESH,
            )
            copy.start()
            copies.append(copy)
        mine = pl.ds(pl.multiple_of(line * UNIT, 8), UNIT)
        dst[mine, :] = src[mine, :]
        return copies

    def total(ref):
        return (ref[0:UNIT, :] + ref[UNIT : 2 * UNIT, :]) + (
            ref[2 * UNIT : 3 * UNIT, :] + ref[3 * UNIT : 4 * UNIT, :]
        )

    swap_s = swap_half(part_s, core_s, 0)
    swap_r = swap_half(part_r, core_r, 1)
    swap_s.wait()
    add_half(part_s, core_s, runs_s)
    lines_s = to_lines(runs_s, from_s, 2)
    for copy in lines_s:
        copy.wait()

    share = total(from_s)
    for x in range(3):
        to_rows[pl.ds(x, SHARE, stride=8), :] = share[SHARE * x : SHARE * x + SHARE]
    planes_of, z = peers(me)
    even = z % 2 == 0
    extra = jnp.logical_and(me < 32, z == 1)
    holder = jnp.logical_or(even, extra)
    row = jnp.where(even, (me // 8) * 4 + z // 2, 32 + me // 8)

    def send_row(to, r):
        pltpu.make_async_remote_copy(
            src_ref=to_rows.at[pl.ds(pl.multiple_of(r * 8, 8), 3)],
            dst_ref=at_rows.at[pl.ds(pl.multiple_of(me * 8, 8), 3)],
            send_sem=send_sems.at[7],
            recv_sem=recv_sems.at[7],
            device_id={"grid": to},
            device_id_type=MESH,
        ).start()

    def send_rows(s, carry):
        half = (z // 2 + s) % 4
        for i in range(1, 8):
            send_row(planes_of[i] + 2 * half, planes_of[i] // 2 + half)

        @pl.when(jnp.logical_or(s > 0, z % 2 == 1))
        def _():
            send_row(planes_of[0] + 2 * half, planes_of[0] // 2 + half)

        return carry

    lax.fori_loop(0, 4, send_rows, 0)
    for i in range(4):
        column = ((me // 8) % 4 + i) % 4

        @pl.when(me != column * 8 + 1)
        def _():
            send_row(column * 8 + 1, 32 + column)

    swap_r.wait()
    add_half(part_r, core_r, runs_r)
    lines_r = to_lines(runs_r, from_r, 5)

    def gather_start(ref, k):
        def push(other, device, sem):
            unit = ref.at[pl.ds(pl.multiple_of(core * HALF + other * UNIT, 8), UNIT)]
            copy = pltpu.make_async_remote_copy(
                src_ref=unit,
                dst_ref=unit,
                send_sem=band_send.at[sem],
                recv_sem=band_recv.at[sem],
                device_id=device,
                device_id_type=MESH,
            )
            copy.start()
            return copy

        copies = [push(line, {"band": 2 * other + core}, k + i) for i, other in enumerate(others)]
        copies.append(push(line, sibling, k + 3))
        return push, copies, k + 4

    def gather_finish(started):
        push, copies, k = started
        passed = []
        for i in range(3):
            copies[i].wait()
            passed.append(push(others[2 - i], sibling, k + i))
        for copy in [copies[3]] + passed:
            copy.wait()

    place = pl.ds(pl.multiple_of(core * HALF + line * UNIT, 8), UNIT)
    @pl.when(holder)
    def _():
        at_rows[pl.ds(pl.multiple_of(me * 8, 8), 8), :] = to_rows[
            pl.ds(pl.multiple_of(row * 8, 8), 8), :
        ]
        drain(at_rows, 3, recv_sems.at[7])
        lines = jnp.concatenate([at_rows[pl.ds(x, G, stride=8), :] for x in range(3)], axis=0)
        spectrum = left_fine(hx_ref[...], lines)
        kx = lax.broadcasted_iota(jnp.int32, (N, 128), 0)
        lane = lax.broadcasted_iota(jnp.int32, (N, 128), 1)
        pair = 12 * band + row - 24
        wide = row < 24
        right = lane >= 64
        ky = jnp.where(wide, 24 * band + row, jnp.where(right, pair + 96, pair))
        kz = jnp.where(wide, lane, jnp.where(right, lane + 64, lane + 128))
        fx, fy, fz = frequency(kx), frequency(ky), frequency(kz)
        kk = fx * fx + fy * fy + fz * fz
        kernel = jnp.where(kk > 0, (N * math.sqrt(N) / 16.0) / (kk + 1.0), 0.0)
        result = left_mul(hxt_ref[...], kernel * spectrum)
        for x in range(3):
            back_rows[pl.ds(x, G, stride=8), :] = result[64 * x : 64 * x + 64]

        def send_back(to):
            pltpu.make_async_remote_copy(
                src_ref=back_rows.at[pl.ds(pl.multiple_of(to * 8, 8), 3)],
                dst_ref=got_rows.at[pl.ds(pl.multiple_of(row * 8, 8), 3)],
                send_sem=send_sems.at[8],
                recv_sem=recv_sems.at[8],
                device_id={"grid": to},
                device_id_type=MESH,
            ).start()

        for_peers(me, send_back)
        got_rows[pl.ds(pl.multiple_of(row * 8, 8), 8), :] = back_rows[
            pl.ds(pl.multiple_of(me * 8, 8), 8), :
        ]

    def drain_rows(sem):
        @pl.when(holder)
        def _():
            span = to_rows.at[pl.ds(0, 35 * 3)]
            pltpu.make_async_copy(span, span, sem).wait()

        @pl.when(jnp.logical_not(holder))
        def _():
            span = to_rows.at[pl.ds(0, 36 * 3)]
            pltpu.make_async_copy(span, span, sem).wait()

    for copy in lines_r:
        copy.wait()
    rho_share = total(from_r)
    root = jnp.exp(jnp.log(jnp.maximum(rho_share, 1e-37)) * (1.0 / 3.0))
    all_r[place, :] = -XC_FACTOR * jnp.where(rho_share > 0, root, 0.0)
    gather_r = gather_start(all_r, 8)

    drain_rows(recv_sems.at[8])
    for x in range(3):
        all_s[pl.ds(pl.multiple_of(core * HALF + line * UNIT + SHARE * x, 8), SHARE), :] = got_rows[
            pl.ds(x, SHARE, stride=8), :
        ]
    gather_s = gather_start(all_s, 15)
    gather_finish(gather_r)
    gather_finish(gather_s)

    def unpack(ref, x):
        wide = []
        for b in range(8):
            base = (((b % 2) * 4 + b // 2) * 3 + x) * SHARE
            wide.append(ref[base : base + 24, :])
            pairs[12 * b : 12 * b + 12, :] = ref[base + 24 : base + 36, :]
        tail = pairs[...]
        tail = jnp.concatenate([tail[:, :64], tail[:, 64:]], axis=0)
        return jnp.concatenate([jnp.concatenate(wide, axis=0), tail], axis=1)

    for x in range(3):
        spectrum = unpack(all_s, x)
        new_pot[x] = right_mul(left_mul(table_h, spectrum), table_h) + unpack(all_r, x)

    drain(out_a, WIDE, send_sems.at[0])
    drain(out_a, last, send_sems.at[1])
    for k, ref in ((2, out_u), (4, out_c)):
        drain(ref, WIDE, send_sems.at[k])
        drain(ref, 9, send_sems.at[k + 1])
    drain_rows(send_sems.at[7])
    store.wait()

    @pl.when(holder)
    def _():
        drain(back_rows, 3, send_sems.at[8])


def hand_over(fresh, pot, fresh_out, pot_out, fresh_held, pot_held, in_sems, out_sems):
    moves = [(fresh.at[0, c, x], fresh_held.at[c, x], fresh_out.at[0, c, x]) for c in range(2) for x in range(3)]
    moves += [(pot.at[x], pot_held.at[x], pot_out.at[x]) for x in range(3)]
    loads = [pltpu.make_async_copy(src, held, in_sems.at[i]) for i, (src, held, _) in enumerate(moves)]
    stores = [pltpu.make_async_copy(held, dst, out_sems.at[i]) for i, (_, held, dst) in enumerate(moves)]
    for load in loads:
        load.start()
    for load, store in zip(loads, stores):
        load.wait()
        store.start()
    for store in stores:
        store.wait()


def local(orbitals, occupations, ion, hxc):
    table = circulant()
    cas = hartley()
    order = np.arange(N)
    order = 3 * (order % G) + order // G
    vmem = pl.BlockSpec(memory_space=pltpu.VMEM)
    hbm = pl.BlockSpec(memory_space=pl.ANY)
    f32 = jnp.float32
    shapes = (jax.ShapeDtypeStruct((1, 2, 3, N, N), f32), jax.ShapeDtypeStruct((3, N, N), f32))
    slots = lambda rows: pltpu.VMEM((rows, 128), f32)
    fresh, new_pot = pl.pallas_call(
        propagate,
        out_shape=shapes,
        in_specs=[hbm, pl.BlockSpec(memory_space=pltpu.SMEM)] + [hbm] * 7,
        out_specs=(hbm, vmem),
        scratch_shapes=[
            pltpu.VMEM((2, 3, N, N), f32),
            pltpu.VMEM((3, N, N), f32),
            pltpu.VMEM((3, N, N), f32),
            pltpu.VMEM((2, N, N), jnp.bfloat16),
            pltpu.VMEM((2, N, N), jnp.bfloat16),
            pltpu.VMEM((3, N, N), jnp.bfloat16),
            pltpu.VMEM((3, N, N), jnp.bfloat16),
            pltpu.VMEM((2, N, N), jnp.bfloat16),
            pltpu.VMEM((2, 3, N, N), f32),
            slots(G * SLOT),
            slots(G * SLOT),
            slots(G * SLOT),
            slots(G * SLOT),
            slots(G * SLOT),
            slots(G * SLOT),
            pltpu.VMEM((2, VROWS * 64, 128), f32),
            pltpu.VMEM((3, N, N), f32),
            pltpu.VMEM((2, 3, N, N), f32),
            pltpu.VMEM((2, 3, N, N), f32),
            slots(96),
            slots(2 * HALF),
            slots(2 * HALF),
            slots(HALF),
            slots(HALF),
            slots(HALF),
            slots(HALF),
            slots(HALF),
            slots(HALF),
            slots(SHARE * 8),
            slots(G * 8),
            slots(G * 8),
            slots(SHARE * 8),
            slots(2 * HALF),
            slots(2 * HALF),
            pltpu.SemaphoreType.DMA((9,)),
            pltpu.SemaphoreType.DMA((9,)),
            pltpu.SemaphoreType.DMA((6,)),
            pltpu.SemaphoreType.DMA((9,)),
            pltpu.SemaphoreType.DMA((22,)),
            pltpu.SemaphoreType.DMA((22,)),
        ],
        compiler_params=pltpu.CompilerParams(
            collective_id=1, has_side_effects=True, vmem_limit_bytes=56 << 20
        ),
        name="propagate",
    )(
        orbitals,
        occupations,
        ion,
        hxc,
        split_table(table),
        split_table(table[order][:, order]),
        split_table(cas, 3),
        split_table(cas[:, order], 3),
        split_table(cas[:, order].T),
    )
    return pl.pallas_call(
        hand_over,
        out_shape=shapes,
        in_specs=[hbm, hbm],
        out_specs=(hbm, hbm),
        scratch_shapes=[
            pltpu.VMEM((2, 3, N, N), f32),
            pltpu.VMEM((3, N, N), f32),
            pltpu.SemaphoreType.DMA((9,)),
            pltpu.SemaphoreType.DMA((9,)),
        ],
        name="hand_over",
    )(fresh, new_pot)


def solution(mesh):
    placed = (
        P("band", None, "grid", None, None),
        P("band"),
        P("grid", None, None),
        P("grid", None, None),
    )
    return jax.shard_map(
        local,
        mesh=mesh,
        in_specs=placed,
        out_specs=(P("band", None, "grid", None, None), P("grid", None, None)),
        check_vma=False,
    )
```

```python
import math

import jax
import jax.numpy as jnp
import numpy as np
from jax import lax
from jax.experimental import pallas as pl
from jax.experimental.pallas import tpu as pltpu
from jax.sharding import PartitionSpec as P

BESSEL_ZERO = 0.8462873527504802
BESSEL_ONE = 0.36884204609417703
BESSEL_TWO = 0.07581776248
XC_FACTOR = 0.98474502
MESH = pl.DeviceIdType.MESH
N = 192
G = 64
SLOT = 40
WIDE = 18
TAIL = 24
VROWS = 7
SHARE = 40
UNIT = 3 * SHARE
HALF = 4 * UNIT


def circulant():
    idx = np.arange(N)
    freq = np.where(idx < N // 2, idx, idx - N).astype(np.float64)
    eigen = 2.0 * freq * freq / (3.0 * (N / 2) ** 2)
    angle = 2.0 * np.pi * ((idx[:, None] * idx[None, :]) % N) / N
    first = (np.cos(angle) @ eigen) / N
    return first[(idx[:, None] - idx[None, :]) % N]


def hartley():
    idx = np.arange(N)
    angle = 2.0 * np.pi * ((idx[:, None] * idx[None, :]) % N) / N
    return (np.cos(angle) + np.sin(angle)) / math.sqrt(N)


def split_table(table, parts=2):
    pieces = []
    for _ in range(parts):
        piece = table.astype(jnp.bfloat16)
        pieces.append(piece)
        table = table - piece.astype(np.float64)
    return np.stack(pieces)


def halves(value):
    high = value.astype(jnp.bfloat16)
    return high, (value - high.astype(jnp.float32)).astype(jnp.bfloat16)


def dot(a, b):
    return jnp.dot(a, b, preferred_element_type=jnp.float32)


def left_mul(table, value):
    high, low = halves(value)
    return dot(table[0], high) + (dot(table[0], low) + dot(table[1], high))


def right_mul(value, table):
    high, low = halves(value)
    return dot(high, table[0]) + (dot(low, table[0]) + dot(high, table[1]))


def thirds(value):
    high, rest = halves(value)
    left = value - high.astype(jnp.float32)
    return high, rest, (left - rest.astype(jnp.float32)).astype(jnp.bfloat16)


def left_fine(table, value):
    high, mid, low = thirds(value)
    small = dot(table[2], high) + dot(table[1], mid) + dot(table[0], low)
    return dot(table[0], high) + (dot(table[1], high) + dot(table[0], mid) + small)


def right_fine(value, table):
    high, mid, low = thirds(value)
    small = dot(high, table[2]) + dot(mid, table[1]) + dot(low, table[0])
    return dot(high, table[0]) + (dot(high, table[1]) + dot(mid, table[0]) + small)


def frequency(idx):
    return jnp.where(idx < N // 2, idx, idx - N).astype(jnp.float32)


def peers(me):
    yh, x, z = me // 32, (me // 8) % 4, me % 8
    planes = [((yh + i % 2) % 2) * 32 + ((x + i // 2) % 4) * 8 for i in range(8)]
    return planes, z


def for_peers(me, act):
    planes, z = peers(me)
    for i in range(1, 8):
        act(planes[i] + z)

    def step(s, carry):
        at = (z + 5 * s) % 8
        for i in range(8):
            act(planes[i] + at)
        return carry

    lax.fori_loop(1, 8, step, 0)


def scatter(me, src, dst, first, rows, send_sem, recv_sem):
    landing = dst.at[pl.ds(pl.multiple_of(me * SLOT + first, 8), rows)]

    def send(to):
        pltpu.make_async_remote_copy(
            src_ref=src.at[pl.ds(pl.multiple_of(to * SLOT + first, 8), rows)],
            dst_ref=landing,
            send_sem=send_sem,
            recv_sem=recv_sem,
            device_id={"grid": to},
            device_id_type=MESH,
        ).start()

    for_peers(me, send)


def own(me, src, dst, first, rows, sem):
    copy = pltpu.make_async_copy(
        src.at[pl.ds(pl.multiple_of(me * SLOT + first, 8), rows)],
        dst.at[pl.ds(pl.multiple_of(me * SLOT + first, 8), rows)],
        sem,
    )
    copy.start()
    return copy


def drain(ref, rows, sem):
    span = ref.at[pl.ds(0, (G - 1) * rows)]
    pltpu.make_async_copy(span, span, sem).wait()


def propagate(
    psi_in, occ, ion_in, hxc_in, d_in, dp_in, h_in, hx_in, hxt_in, fresh_out, new_pot,
    psi, ion, hxc, d_ref, dp_ref, h_ref, hx_ref, hxt_ref, fresh,
    out_a, in_a, out_u, in_u, out_c, in_c, vshare, pot, once, twice,
    pairs, part_s, part_r, core_s, core_r, runs_s, runs_r, from_s, from_r,
    to_rows, at_rows, back_rows, got_rows, all_s, all_r,
    send_sems, recv_sems, own_sems, load_sems, band_send, band_recv,
):
    me = lax.axis_index("grid")
    band = lax.axis_index("band")
    core = band % 2
    line = band // 2
    sibling = {"band": band + 1 - 2 * core}
    others = [(line + d) % 4 for d in range(1, 4)]

    loads = [
        pltpu.make_async_copy(src, dst, load_sems.at[i])
        for i, (src, dst) in enumerate(
            [
                (psi_in.at[0], psi),
                (ion_in, ion),
                (hxc_in, hxc),
                (d_in, d_ref),
                (dp_in, dp_ref),
                (h_in, h_ref),
                (hx_in, hx_ref),
                (hxt_in, hxt_ref),
            ]
        )
    ]
    for load in loads:
        load.start()

    barrier = pltpu.get_barrier_semaphore()

    def greet(to):
        pl.semaphore_signal(barrier, inc=1, device_id={"grid": to}, device_id_type=MESH)

    for_peers(me, greet)
    pl.semaphore_signal(barrier, inc=1, device_id=sibling, device_id_type=MESH)
    for other in others:
        pl.semaphore_signal(
            barrier, inc=1, device_id={"band": 2 * other + core}, device_id_type=MESH
        )

    def at(x, kind, j):
        return (TAIL if kind == 2 else 9 * kind) + 3 * x + j

    loads[0].wait()
    for x in range(3):
        for kind in range(2):
            for j in range(3):
                out_a[pl.ds(at(x, kind, j), G, stride=SLOT), :] = psi[
                    kind, x, 64 * j : 64 * j + 64, :128
                ]

    pl.semaphore_wait(barrier, G + 3)
    last = 9 + VROWS
    mine_wide = own(me, out_a, in_a, 0, WIDE, own_sems.at[0])
    scatter(me, out_a, in_a, 0, WIDE, send_sems.at[0], recv_sems.at[0])

    for x in range(3):
        value = jnp.concatenate([psi[0, x, :, 128:], psi[1, x, :, 128:]], axis=1)
        for j in range(3):
            out_a[pl.ds(at(x, 2, j), G, stride=SLOT), :] = value[64 * j : 64 * j + 64]
    loads[1].wait()
    loads[2].wait()
    blocks = []
    tails = []
    for x in range(3):
        value = ion[x] + hxc[x]
        pot[x] = value - 1.0
        for j in range(3):
            blocks.append(value[64 * j : 64 * j + 64, :128])
            tails.append(value[64 * j : 64 * j + 64, 128:])
    tails.append(tails[8])
    for i in range(5):
        blocks.append(jnp.concatenate([tails[2 * i], tails[2 * i + 1]], axis=1))
    for i in range(VROWS):
        out_a[pl.ds(TAIL + 9 + i, G, stride=SLOT), :] = jnp.where(
            core == 0, blocks[i], blocks[VROWS + i]
        )
    mine_tail = own(me, out_a, in_a, TAIL, last, own_sems.at[1])
    scatter(me, out_a, in_a, TAIL, last, send_sems.at[1], recv_sems.at[1])
    for load in loads[3:]:
        load.wait()

    def inside(i, carry):
        c, x = i // 3, i % 3
        table = d_ref[...]
        value = psi[c, x]
        v = pot[x]
        a = left_mul(table, value) + right_mul(value, table) + v * value
        once[c, x] = a
        twice[c, x] = left_mul(table, a) + right_mul(a, table) + v * a
        return carry

    lax.fori_loop(0, 6, inside, 0)

    def columns(ref, kind):
        return jnp.concatenate(
            [
                jnp.concatenate(
                    [ref[pl.ds(at(x, kind, j), G, stride=SLOT), :] for j in range(3)], axis=1
                )
                for x in range(3)
            ],
            axis=0,
        )

    def spread(ref, kind, value):
        for x in range(3):
            for j in range(3):
                ref[pl.ds(at(x, kind, j), G, stride=SLOT), :] = value[
                    64 * x : 64 * x + 64, 128 * j : 128 * j + 128
                ]

    table = dp_ref[...]
    mine_wide.wait()
    drain(in_a, WIDE, recv_sems.at[0])
    for kind in range(2):
        spread(out_u, kind, left_mul(table, columns(in_a, kind)))
    mine_wide = own(me, out_u, in_u, 0, WIDE, own_sems.at[2])
    scatter(me, out_u, in_u, 0, WIDE, send_sems.at[2], recv_sems.at[2])

    mine_tail.wait()
    drain(in_a, last, recv_sems.at[1])
    spread(out_u, 2, left_mul(table, columns(in_a, 2)))
    mine_tail = own(me, out_u, in_u, TAIL, 9, own_sems.at[3])
    scatter(me, out_u, in_u, TAIL, 9, send_sems.at[3], recv_sems.at[3])

    for i in range(VROWS):
        vshare[core, pl.ds(64 * i, 64), :] = in_a[pl.ds(TAIL + 9 + i, G, stride=SLOT), :]
    swap = pltpu.make_async_remote_copy(
        src_ref=vshare.at[core],
        dst_ref=vshare.at[core],
        send_sem=send_sems.at[6],
        recv_sem=recv_sems.at[6],
        device_id=sibling,
        device_id_type=MESH,
    )
    swap.start()
    swap.wait()

    def vblock(i):
        half, row = i // VROWS, i % VROWS
        return vshare[half, 64 * row : 64 * row + 64, :]

    def vtail(i):
        pair = vblock(9 + i // 2)
        piece = pair[:, :64] if i % 2 == 0 else pair[:, 64:]
        return jnp.concatenate([piece, piece], axis=1)

    def vcolumns(kind):
        pick = vtail if kind == 2 else vblock
        return jnp.concatenate(
            [jnp.concatenate([pick(3 * x + j) for j in range(3)], axis=1) for x in range(3)], axis=0
        )

    for kind in range(3):
        value = columns(out_u, kind) + (vcolumns(kind) - 1.0) * columns(in_a, kind)
        spread(out_c, kind, left_mul(table, value))
    mine_c = [
        own(me, out_c, in_c, 0, WIDE, own_sems.at[4]),
        own(me, out_c, in_c, TAIL, 9, own_sems.at[5]),
    ]
    scatter(me, out_c, in_c, 0, WIDE, send_sems.at[4], recv_sems.at[4])
    scatter(me, out_c, in_c, TAIL, 9, send_sems.at[5], recv_sems.at[5])

    def planes(ref, x):
        kinds = [
            jnp.concatenate(
                [ref[pl.ds(at(x, kind, j), G, stride=SLOT), :] for j in range(3)], axis=0
            )
            for kind in range(3)
        ]
        re = jnp.concatenate([kinds[0], kinds[2][:, :64]], axis=1)
        im = jnp.concatenate([kinds[1], kinds[2][:, 64:]], axis=1)
        return re, im

    mine_wide.wait()
    mine_tail.wait()
    drain(in_u, WIDE, recv_sems.at[2])
    drain(in_u, 9, recv_sems.at[3])
    inner = d_ref[...]
    alpha = BESSEL_ZERO + 2.0 * BESSEL_TWO
    for x in range(3):
        ure, uim = planes(in_u, x)
        v = pot[x]
        second_re = twice[0, x] + 2.0 * (left_mul(inner, ure) + right_mul(ure, inner)) + v * ure
        second_im = twice[1, x] + 2.0 * (left_mul(inner, uim) + right_mul(uim, inner)) + v * uim
        first_re = once[0, x] + ure
        first_im = once[1, x] + uim
        once[0, x] = alpha * psi[0, x] + 2.0 * BESSEL_ONE * first_im - 4.0 * BESSEL_TWO * second_re
        once[1, x] = alpha * psi[1, x] - 2.0 * BESSEL_ONE * first_re - 4.0 * BESSEL_TWO * second_im

    for copy in mine_c:
        copy.wait()
    drain(in_c, WIDE, recv_sems.at[4])
    drain(in_c, 9, recv_sems.at[5])
    table_h = h_ref[...]
    weight = occ[0]

    def pack(ref, x, value):
        pairs[...] = jnp.concatenate([value[:96, 128:], value[96:, 128:]], axis=1)
        for b in range(8):
            base = (((b % 2) * 4 + b // 2) * 3 + x) * SHARE
            ref[base : base + 24, :] = value[24 * b : 24 * b + 24, :128]
            ref[base + 24 : base + 36, :] = pairs[12 * b : 12 * b + 12, :]
            ref[base + 36 : base + 40, :] = jnp.zeros((4, 128), jnp.float32)

    for x in range(3):
        cre, cim = planes(in_c, x)
        re = once[0, x] - 4.0 * BESSEL_TWO * cre
        im = once[1, x] - 4.0 * BESSEL_TWO * cim
        fresh[0, x] = re
        fresh[1, x] = im
        rho = weight * (re * re + im * im)
        pack(part_r, x, rho)
        pack(part_s, x, right_fine(left_fine(table_h, rho), table_h))

    store = pltpu.make_async_copy(fresh, fresh_out.at[0], load_sems.at[8])
    store.start()

    def swap_half(src, dst, k):
        half = pl.multiple_of((1 - core) * HALF, 8)
        copy = pltpu.make_async_remote_copy(
            src_ref=src.at[pl.ds(half, HALF)],
            dst_ref=dst,
            send_sem=band_send.at[k],
            recv_sem=band_recv.at[k],
            device_id=sibling,
            device_id_type=MESH,
        )
        copy.start()
        return copy

    def add_half(src, dst, out):
        out[...] = src[pl.ds(pl.multiple_of(core * HALF, 8), HALF), :] + dst[...]

    def to_lines(src, dst, k):
        copies = []
        for i, other in enumerate(others):
            copy = pltpu.make_async_remote_copy(
                src_ref=src.at[pl.ds(pl.multiple_of(other * UNIT, 8), UNIT)],
                dst_ref=dst.at[pl.ds(pl.multiple_of(line * UNIT, 8), UNIT)],
                send_sem=band_send.at[k + i],
                recv_sem=band_recv.at[k + i],
                device_id={"band": 2 * other + core},
                device_id_type=MESH,
            )
            copy.start()
            copies.append(copy)
        mine = pl.ds(pl.multiple_of(line * UNIT, 8), UNIT)
        dst[mine, :] = src[mine, :]
        return copies

    def total(ref):
        return (ref[0:UNIT, :] + ref[UNIT : 2 * UNIT, :]) + (
            ref[2 * UNIT : 3 * UNIT, :] + ref[3 * UNIT : 4 * UNIT, :]
        )

    swap_s = swap_half(part_s, core_s, 0)
    swap_r = swap_half(part_r, core_r, 1)
    swap_s.wait()
    add_half(part_s, core_s, runs_s)
    lines_s = to_lines(runs_s, from_s, 2)
    for copy in lines_s:
        copy.wait()

    share = total(from_s)
    for x in range(3):
        to_rows[pl.ds(x, SHARE, stride=8), :] = share[SHARE * x : SHARE * x + SHARE]
    planes_of, z = peers(me)
    even = z % 2 == 0
    extra = jnp.logical_and(me < 32, z == 1)
    holder = jnp.logical_or(even, extra)
    row = jnp.where(even, (me // 8) * 4 + z // 2, 32 + me // 8)

    def send_row(to, r):
        pltpu.make_async_remote_copy(
            src_ref=to_rows.at[pl.ds(pl.multiple_of(r * 8, 8), 3)],
            dst_ref=at_rows.at[pl.ds(pl.multiple_of(me * 8, 8), 3)],
            send_sem=send_sems.at[7],
            recv_sem=recv_sems.at[7],
            device_id={"grid": to},
            device_id_type=MESH,
        ).start()

    def send_rows(s, carry):
        half = (z // 2 + s) % 4
        for i in range(1, 8):
            send_row(planes_of[i] + 2 * half, planes_of[i] // 2 + half)

        @pl.when(jnp.logical_or(s > 0, z % 2 == 1))
        def _():
            send_row(planes_of[0] + 2 * half, planes_of[0] // 2 + half)

        return carry

    lax.fori_loop(0, 4, send_rows, 0)
    for i in range(4):
        column = ((me // 8) % 4 + i) % 4

        @pl.when(me != column * 8 + 1)
        def _():
            send_row(column * 8 + 1, 32 + column)

    swap_r.wait()
    add_half(part_r, core_r, runs_r)
    lines_r = to_lines(runs_r, from_r, 5)

    def gather_start(ref, k):
        def push(other, device, sem):
            unit = ref.at[pl.ds(pl.multiple_of(core * HALF + other * UNIT, 8), UNIT)]
            copy = pltpu.make_async_remote_copy(
                src_ref=unit,
                dst_ref=unit,
                send_sem=band_send.at[sem],
                recv_sem=band_recv.at[sem],
                device_id=device,
                device_id_type=MESH,
            )
            copy.start()
            return copy

        copies = [push(line, {"band": 2 * other + core}, k + i) for i, other in enumerate(others)]
        copies.append(push(line, sibling, k + 3))
        return push, copies, k + 4

    def gather_finish(started):
        push, copies, k = started
        passed = []
        for i in range(3):
            copies[i].wait()
            passed.append(push(others[2 - i], sibling, k + i))
        for copy in [copies[3]] + passed:
            copy.wait()

    place = pl.ds(pl.multiple_of(core * HALF + line * UNIT, 8), UNIT)
    @pl.when(holder)
    def _():
        at_rows[pl.ds(pl.multiple_of(me * 8, 8), 8), :] = to_rows[
            pl.ds(pl.multiple_of(row * 8, 8), 8), :
        ]
        drain(at_rows, 3, recv_sems.at[7])
        lines = jnp.concatenate([at_rows[pl.ds(x, G, stride=8), :] for x in range(3)], axis=0)
        spectrum = left_fine(hx_ref[...], lines)
        kx = lax.broadcasted_iota(jnp.int32, (N, 128), 0)
        lane = lax.broadcasted_iota(jnp.int32, (N, 128), 1)
        pair = 12 * band + row - 24
        wide = row < 24
        right = lane >= 64
        ky = jnp.where(wide, 24 * band + row, jnp.where(right, pair + 96, pair))
        kz = jnp.where(wide, lane, jnp.where(right, lane + 64, lane + 128))
        fx, fy, fz = frequency(kx), frequency(ky), frequency(kz)
        kk = fx * fx + fy * fy + fz * fz
        kernel = jnp.where(kk > 0, (N * math.sqrt(N) / 16.0) / (kk + 1.0), 0.0)
        result = left_mul(hxt_ref[...], kernel * spectrum)
        for x in range(3):
            back_rows[pl.ds(x, G, stride=8), :] = result[64 * x : 64 * x + 64]

        def send_back(to):
            pltpu.make_async_remote_copy(
                src_ref=back_rows.at[pl.ds(pl.multiple_of(to * 8, 8), 3)],
                dst_ref=got_rows.at[pl.ds(pl.multiple_of(row * 8, 8), 3)],
                send_sem=send_sems.at[8],
                recv_sem=recv_sems.at[8],
                device_id={"grid": to},
                device_id_type=MESH,
            ).start()

        for_peers(me, send_back)
        got_rows[pl.ds(pl.multiple_of(row * 8, 8), 8), :] = back_rows[
            pl.ds(pl.multiple_of(me * 8, 8), 8), :
        ]

    def drain_rows(sem):
        @pl.when(holder)
        def _():
            span = to_rows.at[pl.ds(0, 35 * 3)]
            pltpu.make_async_copy(span, span, sem).wait()

        @pl.when(jnp.logical_not(holder))
        def _():
            span = to_rows.at[pl.ds(0, 36 * 3)]
            pltpu.make_async_copy(span, span, sem).wait()

    for copy in lines_r:
        copy.wait()
    rho_share = total(from_r)
    root = jnp.exp(jnp.log(jnp.maximum(rho_share, 1e-37)) * (1.0 / 3.0))
    all_r[place, :] = -XC_FACTOR * jnp.where(rho_share > 0, root, 0.0)
    gather_r = gather_start(all_r, 8)

    drain_rows(recv_sems.at[8])
    for x in range(3):
        all_s[pl.ds(pl.multiple_of(core * HALF + line * UNIT + SHARE * x, 8), SHARE), :] = got_rows[
            pl.ds(x, SHARE, stride=8), :
        ]
    gather_s = gather_start(all_s, 15)
    gather_finish(gather_r)
    def unpack(ref, x):
        wide = []
        for b in range(8):
            base = (((b % 2) * 4 + b // 2) * 3 + x) * SHARE
            wide.append(ref[base : base + 24, :])
            pairs[12 * b : 12 * b + 12, :] = ref[base + 24 : base + 36, :]
        tail = pairs[...]
        tail = jnp.concatenate([tail[:, :64], tail[:, 64:]], axis=0)
        return jnp.concatenate([jnp.concatenate(wide, axis=0), tail], axis=1)

    for x in range(3):
        new_pot[x] = unpack(all_r, x)
    gather_finish(gather_s)
    for x in range(3):
        spectrum = unpack(all_s, x)
        new_pot[x] = right_mul(left_mul(table_h, spectrum), table_h) + new_pot[x]

    drain(out_a, WIDE, send_sems.at[0])
    drain(out_a, last, send_sems.at[1])
    for k, ref in ((2, out_u), (4, out_c)):
        drain(ref, WIDE, send_sems.at[k])
        drain(ref, 9, send_sems.at[k + 1])
    drain_rows(send_sems.at[7])
    store.wait()

    @pl.when(holder)
    def _():
        drain(back_rows, 3, send_sems.at[8])


def hand_over(fresh, pot, fresh_out, pot_out, fresh_held, pot_held, in_sems, out_sems):
    moves = [(fresh.at[0, c, x], fresh_held.at[c, x], fresh_out.at[0, c, x]) for c in range(2) for x in range(3)]
    moves += [(pot.at[x], pot_held.at[x], pot_out.at[x]) for x in range(3)]
    loads = [pltpu.make_async_copy(src, held, in_sems.at[i]) for i, (src, held, _) in enumerate(moves)]
    stores = [pltpu.make_async_copy(held, dst, out_sems.at[i]) for i, (_, held, dst) in enumerate(moves)]
    for load in loads:
        load.start()
    for load, store in zip(loads, stores):
        load.wait()
        store.start()
    for store in stores:
        store.wait()


def local(orbitals, occupations, ion, hxc):
    table = circulant()
    cas = hartley()
    order = np.arange(N)
    order = 3 * (order % G) + order // G
    vmem = pl.BlockSpec(memory_space=pltpu.VMEM)
    hbm = pl.BlockSpec(memory_space=pl.ANY)
    f32 = jnp.float32
    shapes = (jax.ShapeDtypeStruct((1, 2, 3, N, N), f32), jax.ShapeDtypeStruct((3, N, N), f32))
    slots = lambda rows: pltpu.VMEM((rows, 128), f32)
    fresh, new_pot = pl.pallas_call(
        propagate,
        out_shape=shapes,
        in_specs=[hbm, pl.BlockSpec(memory_space=pltpu.SMEM)] + [hbm] * 7,
        out_specs=(hbm, vmem),
        scratch_shapes=[
            pltpu.VMEM((2, 3, N, N), f32),
            pltpu.VMEM((3, N, N), f32),
            pltpu.VMEM((3, N, N), f32),
            pltpu.VMEM((2, N, N), jnp.bfloat16),
            pltpu.VMEM((2, N, N), jnp.bfloat16),
            pltpu.VMEM((3, N, N), jnp.bfloat16),
            pltpu.VMEM((3, N, N), jnp.bfloat16),
            pltpu.VMEM((2, N, N), jnp.bfloat16),
            pltpu.VMEM((2, 3, N, N), f32),
            slots(G * SLOT),
            slots(G * SLOT),
            slots(G * SLOT),
            slots(G * SLOT),
            slots(G * SLOT),
            slots(G * SLOT),
            pltpu.VMEM((2, VROWS * 64, 128), f32),
            pltpu.VMEM((3, N, N), f32),
            pltpu.VMEM((2, 3, N, N), f32),
            pltpu.VMEM((2, 3, N, N), f32),
            slots(96),
            slots(2 * HALF),
            slots(2 * HALF),
            slots(HALF),
            slots(HALF),
            slots(HALF),
            slots(HALF),
            slots(HALF),
            slots(HALF),
            slots(SHARE * 8),
            slots(G * 8),
            slots(G * 8),
            slots(SHARE * 8),
            slots(2 * HALF),
            slots(2 * HALF),
            pltpu.SemaphoreType.DMA((9,)),
            pltpu.SemaphoreType.DMA((9,)),
            pltpu.SemaphoreType.DMA((6,)),
            pltpu.SemaphoreType.DMA((9,)),
            pltpu.SemaphoreType.DMA((22,)),
            pltpu.SemaphoreType.DMA((22,)),
        ],
        compiler_params=pltpu.CompilerParams(
            collective_id=1, has_side_effects=True, vmem_limit_bytes=56 << 20
        ),
        name="propagate",
    )(
        orbitals,
        occupations,
        ion,
        hxc,
        split_table(table),
        split_table(table[order][:, order]),
        split_table(cas, 3),
        split_table(cas[:, order], 3),
        split_table(cas[:, order].T),
    )
    return pl.pallas_call(
        hand_over,
        out_shape=shapes,
        in_specs=[hbm, hbm],
        out_specs=(hbm, hbm),
        scratch_shapes=[
            pltpu.VMEM((2, 3, N, N), f32),
            pltpu.VMEM((3, N, N), f32),
            pltpu.SemaphoreType.DMA((9,)),
            pltpu.SemaphoreType.DMA((9,)),
        ],
        name="hand_over",
    )(fresh, new_pot)


def solution(mesh):
    placed = (
        P("band", None, "grid", None, None),
        P("band"),
        P("grid", None, None),
        P("grid", None, None),
    )
    return jax.shard_map(
        local,
        mesh=mesh,
        in_specs=placed,
        out_specs=(P("band", None, "grid", None, None), P("grid", None, None)),
        check_vma=False,
    )
```
